32 devices in a mesh: expert: 8 (over y, x, core), tensor: 4 (over z).
Axes of the slice: x: 2, y: 2, z: 4, core: 2. Of those that a mesh axis runs over, the one named last changes fastest.
Arguments:
- tokens: bfloat16 [1024, 6144], P('expert', 'tensor'), may hold values from -6 to 6
- expert_ids: int32 [1024, 2], P('expert'), may hold values from 0 to 7, all different within a row; in each aligned block of 128 rows (0 to 127, 128 to 255, ...) at most 48 rows name the same one
- gate_fixed: int32 [1024, 2], P('expert'), may hold values from 4096 to 65535
- w_gate: bfloat16 [8, 4096, 6144], P('expert', None, 'tensor'), may hold values from -0.078125 to 0.078125
- w_up: bfloat16 [8, 4096, 6144], P('expert', None, 'tensor'), may hold values from -0.078125 to 0.078125
- w_down: bfloat16 [8, 4096, 6144], P('expert', None, 'tensor'), may hold values from -0.0625 to 0.0625
Outputs:
- mixed: bfloat16 [1024, 6144], P('expert', 'tensor')
The draws below stay inside these ranges and needn't reach their ends.
Inputs may be any that keep to these rules, and one draw needn't show every extreme that they name: `expert_ids`: each row names 2 different experts. Among the 128 rows of one sequence shard (aligned blocks), no expert is named by more than 48 rows, a bound that some block reaches.
All inputs are finite; a program needn't handle non-finite values.
Results may differ from the reference program's by a relative error of at most 0.0064.
Values may be sent and summed in bfloat16 or wider, within the bound.
A program may use at most 128 MiB of HBM per device.

```python
import math
import jax
import jax.numpy as jnp
import numpy as np
from jax import lax

D = 6144
FFW = 8192
ROUTED = 8
EXPERTS = 4
TOP = 2
TOK_SH = 128
CAP = 48
QUART = 2
FQ = 4096
DT = 1536
TOKENS = 1024
N_EXPERT = 8


def set_ends(entries, stream_key, least, largest):
    place = [jax.random.randint(jax.random.fold_in(stream_key, axis), (), 0, length) for axis, length in enumerate(entries.shape)]
    longest = entries.shape.index(max(entries.shape))
    beside = place[:longest] + [(place[longest] + 1) % entries.shape[longest]] + place[longest + 1:]
    return entries.at[tuple(place)].set(least).at[tuple(beside)].set(largest)


def steps_of(own_key, extent, cuts, low, high):
    factor_of, own = 1.0, jax.random.fold_in(own_key, 6)
    for dim, blocks in cuts:
        draws = jnp.exp(jax.random.uniform(jax.random.fold_in(own, dim), (blocks,), jnp.float32, low / len(cuts), high / len(cuts)))
        factor_of = factor_of * jnp.repeat(draws, extent[dim] // blocks).reshape([-1 if axis == dim else 1 for axis in range(len(extent))])
    return factor_of


def assign_block(stream_key, own, number, rows, number_of, top, limit, slope):
    order = jax.random.permutation(stream_key, number_of)
    packed, ordinary = shares(number_of, rows * top, limit, slope, True), shares(number_of, rows * top, limit, slope, False)
    places = jnp.arange(number_of)

    def named(tallies, rotation):
        used = int((tallies > 0).sum())
        fixed = max(1, used // 4)
        moved = fixed + (places - fixed + rotation * (used - fixed)) % max(1, number_of - fixed)
        return jnp.zeros((number_of,), jnp.int32).at[order[jnp.where(places < fixed, places, moved)]].set(jnp.asarray(tallies, jnp.int32))

    tallies = jnp.where(number % 4 == 0, named(packed, number // 4), named(ordinary, number - number // 4 - 1))
    mixed = jax.random.permutation(jax.random.fold_in(own, 3), number_of)
    source_of, receiver = mixed[0:number_of // 2 * 2:2], mixed[1:number_of // 2 * 2:2]
    slack = jnp.minimum(tallies[source_of] - 1, limit - tallies[receiver]) // 2
    slack = jnp.where((source_of == order[0]) | (receiver == order[0]) | (tallies[receiver] == 0), 0, jnp.maximum(slack, 0))
    moved = jax.random.randint(jax.random.fold_in(own, 4), (number_of // 2,), 0, 1 << 20) % (slack + 1)
    tallies = tallies.at[source_of].add(-moved).at[receiver].add(moved)
    labels = jnp.searchsorted(jnp.cumsum(tallies), jnp.arange(rows * top), side="right").astype(jnp.int32)
    listing = labels.reshape(top, rows).T
    listing = listing[jax.random.permutation(jax.random.fold_in(own, 1), rows)]
    rotation = jax.random.randint(jax.random.fold_in(own, 2), (rows, 1), 0, top)
    return jnp.take_along_axis(listing, (jnp.arange(top)[None, :] + rotation) % top, axis=1)


def shares(amount, total, most, slope, full):
    weights = [(1 << 20) // math.isqrt(standing ** slope) + 1 for standing in range(1, amount + 1)]
    largest = most if full else min(most, max(-(-total // amount), total * weights[0] // sum(weights)))
    least = 1 if total - largest >= amount - 1 else 0
    given, spare = [largest] + [least] * (amount - 1), total - largest - least * (amount - 1)
    while spare > 0:
        movable = [i for i in range(1, amount) if given[i] < largest] or [i for i in range(1, amount) if given[i] < most]
        mass, left = sum([weights[i] for i in movable]), spare
        for i in movable:
            more = min(most - given[i], max(1, left * weights[i] // mass), spare)
            given[i] = given[i] + more
            spare = spare - more
    return np.array(given)


def bell_draw(key, shape, spread, bound, shards=(), kind=jnp.bfloat16):
    entries = jax.random.normal(key, shape, jnp.float32) * spread
    if len(shards) > 0:
        entries = steps_of(key, shape, shards, -0.22, 0.18) * entries
    return jnp.clip(entries, min=-bound, max=bound).astype(kind)


def setup_inputs(seed: int = 0) -> dict:
    keys = jax.random.split(jax.random.key(seed), 7)
    tokens = bell_draw(keys[0], (TOKENS, D), 1.0, 6.0, ((0, 8), (1, 4)))
    expert_ids_keys = jax.random.split(jax.random.fold_in(keys[1], 1), TOKENS // TOK_SH)
    expert_ids_turns = jax.random.permutation(jax.random.fold_in(keys[1], 3), TOKENS // TOK_SH)
    expert_ids = jax.vmap(lambda own, number: assign_block(jax.random.fold_in(keys[1], 2), own, number, TOK_SH, ROUTED, TOP, CAP, 2))(expert_ids_keys, expert_ids_turns).reshape((TOKENS, TOP))
    gate_fixed = set_ends(jax.random.randint(keys[2], (TOKENS, TOP), 4096, 65536), jax.random.fold_in(keys[2], 1), 4096, 65535).astype(jnp.int32)
    w_gate = bell_draw(keys[3], (QUART * EXPERTS, FQ, D), D ** -0.5, 0.078125, ((0, 8), (2, 4)))
    w_up = bell_draw(keys[4], (QUART * EXPERTS, FQ, D), D ** -0.5, 0.078125, ((0, 8), (2, 4)))
    w_down = bell_draw(keys[5], (QUART * EXPERTS, FQ, D), FFW ** -0.5, 0.0625, ((0, 8), (2, 4)))
    return dict(tokens=tokens, expert_ids=expert_ids, gate_fixed=gate_fixed, w_gate=w_gate, w_up=w_up, w_down=w_down)


def expert_rows(token_blocks, gate_matrix, up_matrix, down_matrix):
    gate_blocks = gate_matrix.reshape(FFW, D // DT, DT)
    up_blocks = up_matrix.reshape(FFW, D // DT, DT)
    contract = (((1,), (1,)), ((), ()))

    def add_block(running, block_index):
        gate_sum, up_sum = running
        token_part = lax.dynamic_index_in_dim(token_blocks, block_index, 1, keepdims=False)
        gate_part = lax.dynamic_index_in_dim(gate_blocks, block_index, 1, keepdims=False)
        up_part = lax.dynamic_index_in_dim(up_blocks, block_index, 1, keepdims=False)
        gate_term = lax.dot_general(token_part, gate_part, contract, preferred_element_type=jnp.float32)
        up_term = lax.dot_general(token_part, up_part, contract, preferred_element_type=jnp.float32)
        gate_term = lax.optimization_barrier(gate_term.astype(jnp.bfloat16)).astype(jnp.float32)
        up_term = lax.optimization_barrier(up_term.astype(jnp.bfloat16)).astype(jnp.float32)
        return (gate_sum + gate_term, up_sum + up_term), None

    empty_sum = jnp.zeros((token_blocks.shape[0], FFW), jnp.float32)
    block_list = jnp.arange(D // DT, dtype=jnp.int32)
    (gate_sum, up_sum), _ = lax.scan(add_block, (empty_sum, empty_sum), block_list)
    hidden = (jax.nn.silu(gate_sum) * up_sum).astype(jnp.bfloat16)
    return jnp.dot(hidden, down_matrix, preferred_element_type=jnp.float32)


def reference(tokens, expert_ids, gate_fixed, w_gate, w_up, w_down):
    quarters = N_EXPERT // EXPERTS
    slots = N_EXPERT * CAP

    def regroup(weight_arr):
        return weight_arr.reshape(quarters, EXPERTS, FQ, D).transpose(1, 0, 2, 3).reshape(EXPERTS, FFW, D)

    token_blocks = tokens.reshape(TOKENS, D // DT, DT)
    slot_iota = jnp.arange(slots, dtype=jnp.int32)

    def one_expert(total, weight_set):
        gate_matrix, up_matrix, down_matrix, which = weight_set
        matched = expert_ids == which
        weight = jnp.sum(jnp.where(matched, gate_fixed, 0), axis=1).astype(jnp.float32) / 65536.0
        hit = jnp.any(matched, axis=1)
        count = jnp.sum(hit.astype(jnp.int32))
        index = jnp.nonzero(hit, size=slots, fill_value=0)[0].astype(jnp.int32)
        row_weight = jnp.where(slot_iota < count, weight[index], jnp.float32(0.0))
        out = expert_rows(token_blocks[index], gate_matrix, up_matrix, down_matrix)
        return total.at[index].add(out * row_weight[:, None]), None

    which_list = jnp.arange(EXPERTS, dtype=jnp.int32)
    start = jnp.zeros((TOKENS, D), jnp.float32)
    mixed, _ = lax.scan(one_expert, start, (regroup(w_gate), regroup(w_up), regroup(w_down), which_list))
    return mixed.astype(jnp.bfloat16)
```

```python
import functools

import jax
import jax.numpy as jnp
from jax import lax
from jax.experimental import pallas as pl
from jax.experimental.pallas import tpu as pltpu
from jax.sharding import PartitionSpec as P

EXPERTS = 4
CAP = 48
MESH = pl.DeviceIdType.MESH
CHUNK = 256
SKEW = 2
LINE = 4
CONTRACT_LAST = (((1,), (1,)), ((), ()))


def line_kernel(
    devices, groups, cap, chunk,
    outgoing, high, low, w_gate, w_up, w_down, mixed,
    gate_v, up_v, down_v, rows, running, term, hidden, total, returned,
    gate_sem, up_sem, down_sem, out_send, out_recv, back_send, back_recv,
    run_send, run_recv, hid_send, hid_recv,
):
    me, at = lax.axis_index("expert"), lax.axis_index("tensor")
    held = outgoing.shape[0]
    half = devices * cap // 2
    count = w_gate.shape[1] // chunk
    last = groups - 1
    place = (last - at, at)
    onward = (at - 1, at + 1)
    before = (at + 1, at - 1)
    ahead = jnp.minimum(place[0], place[1])
    behind = jnp.maximum(place[0], place[1])

    def weight(source, target, sem, c):
        cut = pl.ds(pl.multiple_of(c * chunk, chunk), chunk)
        return pltpu.make_async_copy(source.at[0, cut, :], target.at[cut, :], sem.at[c])

    def start_first(c, carry):
        weight(w_gate, gate_v, gate_sem, c).start()
        weight(w_up, up_v, up_sem, c).start()
        return carry

    def start_second(c, carry):
        weight(w_down, down_v, down_sem, c).start()
        return carry

    lax.fori_loop(0, count, start_first, 0)

    barrier = pltpu.get_barrier_semaphore()
    for k in range(1, devices):
        peer = lax.rem(me + k, devices)
        pl.semaphore_signal(barrier, inc=1, device_id={"expert": peer}, device_id_type=MESH)

    @pl.when(at > 0)
    def _():
        pl.semaphore_signal(barrier, inc=1, device_id={"tensor": at - 1}, device_id_type=MESH)

    @pl.when(at < last)
    def _():
        pl.semaphore_signal(barrier, inc=1, device_id={"tensor": at + 1}, device_id_type=MESH)

    inside = (at > 0) & (at < last)

    @pl.when(inside)
    def _():
        pl.semaphore_wait(barrier, devices + 1)

    @pl.when(jnp.logical_not(inside))
    def _():
        pl.semaphore_wait(barrier, devices - 1 + min(last, 1))

    def block(shard):
        return pl.ds(pl.multiple_of(shard * cap, cap), cap)

    def dispatch(peer):
        return pltpu.make_async_remote_copy(
            src_ref=outgoing.at[lax.rem(peer, held)],
            dst_ref=rows.at[block(me), :],
            send_sem=out_send.at[peer],
            recv_sem=out_recv.at[me],
            device_id={"expert": peer},
            device_id_type=MESH,
        )

    def arrived(peer):
        return pltpu.make_async_remote_copy(
            src_ref=outgoing.at[0],
            dst_ref=rows.at[block(peer), :],
            send_sem=out_send.at[peer],
            recv_sem=out_recv.at[peer],
            device_id={"expert": peer},
            device_id_type=MESH,
        )

    for k in range(1, devices):
        dispatch(lax.rem(me + k, devices)).start()
    lax.fori_loop(0, count, start_second, 0)
    rows[block(me), :] = outgoing[lax.rem(me, held)]
    total[...] = jnp.zeros_like(total)
    for k in range(1, devices):
        arrived(lax.rem(me + devices - k, devices)).wait_recv()

    def run_copy(s, c):
        return pltpu.make_async_remote_copy(
            src_ref=running.at[s, c],
            dst_ref=running.at[s, c],
            send_sem=run_send.at[s, c],
            recv_sem=run_recv.at[s, c],
            device_id={"tensor": onward[s]},
            device_id_type=MESH,
        )

    def hid_copy(s, c):
        return pltpu.make_async_remote_copy(
            src_ref=hidden.at[s, c],
            dst_ref=hidden.at[s, c],
            send_sem=hid_send.at[s, c],
            recv_sem=hid_recv.at[s, c],
            device_id={"tensor": before[s]},
            device_id_type=MESH,
        )

    def step(t, carry):
        fresh = t - SKEW * ahead

        @pl.when((fresh >= 0) & (fresh < count))
        def _():
            weight(w_gate, gate_v, gate_sem, fresh).wait()
            weight(w_up, up_v, up_sem, fresh).wait()

        for s in (0, 1):
            c = t - SKEW * place[s]

            @pl.when((c >= 0) & (c < count))
            def _(s=s, c=c):
                cut = pl.ds(pl.multiple_of(c * chunk, chunk), chunk)
                own = rows[s * half : (s + 1) * half, :]
                term[:, :chunk] = lax.dot_general(
                    own, gate_v[cut, :], CONTRACT_LAST, preferred_element_type=jnp.float32
                )
                term[:, chunk:] = lax.dot_general(
                    own, up_v[cut, :], CONTRACT_LAST, preferred_element_type=jnp.float32
                )

                @pl.when(place[s] == 0)
                def _():
                    running[s, c] = term[...].astype(jnp.bfloat16)
                    run_copy(s, c).start()

                @pl.when((place[s] > 0) & (place[s] < last))
                def _():
                    run_copy(s, c).wait_recv()
                    running[s, c] = (running[s, c].astype(jnp.float32) + term[...]).astype(
                        jnp.bfloat16
                    )
                    run_copy(s, c).start()

                @pl.when(place[s] == last)
                def _():
                    run_copy(s, c).wait_recv()
                    whole = running[s, c].astype(jnp.float32) + term[...]
                    gate, up = whole[:, :chunk], whole[:, chunk:]
                    hidden[s, c] = (gate / (1.0 + jnp.exp(-gate)) * up).astype(jnp.bfloat16)
                    hid_copy(s, c).start()

        for s in (0, 1):
            c = t - 2 * SKEW * last + SKEW * place[s]

            @pl.when((c >= 0) & (c < count) & (place[s] < last))
            def _(s=s, c=c):
                hid_copy(s, c).wait_recv()

                @pl.when(place[s] > 0)
                def _():
                    hid_copy(s, c).start()

        ripe = t - 2 * SKEW * last + SKEW * behind

        @pl.when((ripe >= 0) & (ripe < count))
        def _():
            weight(w_down, down_v, down_sem, ripe).wait()

        for s in (0, 1):
            c = t - 2 * SKEW * last + SKEW * place[s]

            @pl.when((c >= 0) & (c < count))
            def _(s=s, c=c):
                cut = pl.ds(pl.multiple_of(c * chunk, chunk), chunk)
                total[s] += jnp.dot(
                    hidden[s, c], down_v[cut, :], preferred_element_type=jnp.float32
                )

        return carry

    lax.fori_loop(0, count + 2 * SKEW * last, step, 0)

    rows[:half, :] = total[0].astype(jnp.bfloat16)
    rows[half:, :] = total[1].astype(jnp.bfloat16)

    def back(peer):
        return pltpu.make_async_remote_copy(
            src_ref=rows.at[block(peer), :],
            dst_ref=returned.at[block(me), :],
            send_sem=back_send.at[peer],
            recv_sem=back_recv.at[me],
            device_id={"expert": peer},
            device_id_type=MESH,
        )

    def came_back(peer):
        return pltpu.make_async_remote_copy(
            src_ref=rows.at[block(peer), :],
            dst_ref=returned.at[block(peer), :],
            send_sem=back_send.at[peer],
            recv_sem=back_recv.at[peer],
            device_id={"expert": peer},
            device_id_type=MESH,
        )

    for k in range(1, devices):
        back(lax.rem(me + k, devices)).start()
    returned[block(me), :] = rows[block(me), :]

    def drain(c, carry):
        for s in (0, 1):

            @pl.when(place[s] < last)
            def _(s=s):
                run_copy(s, c).wait_send()

            @pl.when(place[s] > 0)
            def _(s=s):
                hid_copy(s, c).wait_send()

        return carry

    lax.fori_loop(0, count, drain, 0)
    for k in range(1, devices):
        dispatch(lax.rem(me + k, devices)).wait_send()
    for k in range(1, devices):
        came_back(lax.rem(me + devices - k, devices)).wait_recv()
    coarse = jnp.dot(high[...], returned[...], preferred_element_type=jnp.float32)
    fine = jnp.dot(low[...], returned[...], preferred_element_type=jnp.float32)
    mixed[...] = ((coarse * 256.0 + fine) * (1.0 / 65536.0)).astype(mixed.dtype)
    for k in range(1, devices):
        back(lax.rem(me + k, devices)).wait_send()


def along_line(outgoing, high, low, w_gate, w_up, w_down, devices, groups, cap):
    token_count, width_part = high.shape[0], outgoing.shape[2]
    hidden_width = w_gate.shape[1]
    chunk = min(CHUNK, hidden_width)
    count = hidden_width // chunk
    half = devices * cap // 2
    in_vmem, in_place = pl.BlockSpec(memory_space=pltpu.VMEM), pl.BlockSpec(memory_space=pl.ANY)
    flops = 2 * 3 * 2 * half * hidden_width * width_part
    return pl.pallas_call(
        functools.partial(line_kernel, devices, groups, cap, chunk),
        out_shape=jax.ShapeDtypeStruct((token_count, width_part), jnp.bfloat16),
        in_specs=[in_vmem] * 3 + [in_place] * 3,
        out_specs=in_vmem,
        scratch_shapes=[
            pltpu.VMEM((hidden_width, width_part), jnp.bfloat16),
            pltpu.VMEM((hidden_width, width_part), jnp.bfloat16),
            pltpu.VMEM((hidden_width, width_part), jnp.bfloat16),
            pltpu.VMEM((2 * half, width_part), jnp.bfloat16),
            pltpu.VMEM((2, count, half, 2 * chunk), jnp.bfloat16),
            pltpu.VMEM((half, 2 * chunk), jnp.float32),
            pltpu.VMEM((2, count, half, chunk), jnp.bfloat16),
            pltpu.VMEM((2, half, width_part), jnp.float32),
            pltpu.VMEM((2 * half, width_part), jnp.bfloat16),
            *[pltpu.SemaphoreType.DMA((count,))] * 3,
            *[pltpu.SemaphoreType.DMA((devices,))] * 4,
            *[pltpu.SemaphoreType.DMA((2, count))] * 4,
        ],
        compiler_params=pltpu.CompilerParams(
            collective_id=0, has_side_effects=True, vmem_limit_bytes=60 * 2**20
        ),
        cost_estimate=pl.CostEstimate(
            flops=flops,
            bytes_accessed=3 * 2 * hidden_width * width_part,
            transcendentals=half * hidden_width,
        ),
    )(outgoing, high, low, w_gate, w_up, w_down)


def by_collectives(outgoing, high, low, w_gate, w_up, w_down, devices, groups, cap):
    width_part = outgoing.shape[2]
    arrived = lax.all_to_all(
        jnp.tile(outgoing, (devices // EXPERTS, 1, 1)), "expert", split_axis=0, concat_axis=0, tiled=True
    )
    total_rows = devices * cap
    rows_in = arrived.reshape(total_rows, width_part)
    hidden_width = w_gate.shape[1]

    def summed(weights):
        product = lax.dot_general(
            rows_in, weights[0], CONTRACT_LAST, preferred_element_type=jnp.float32
        ).astype(jnp.bfloat16)
        parts = lax.all_to_all(product, "tensor", split_axis=0, concat_axis=0, tiled=True)
        parts = parts.reshape(groups, total_rows // groups, hidden_width)
        return jnp.sum(parts.astype(jnp.float32), axis=0)

    hidden = (jax.nn.silu(summed(w_gate)) * summed(w_up)).astype(jnp.bfloat16)
    partial_out = jnp.dot(
        lax.all_gather(hidden, "tensor", axis=0, tiled=True),
        w_down[0],
        preferred_element_type=jnp.float32,
    )
    returned = lax.all_to_all(
        partial_out.reshape(devices, cap, width_part), "expert", split_axis=0, concat_axis=0, tiled=True
    )
    selector = (high.astype(jnp.float32) * 256.0 + low.astype(jnp.float32)) / 65536.0
    mixed = jnp.dot(
        selector, returned.reshape(total_rows, width_part), precision=lax.Precision.HIGHEST
    )
    return mixed.astype(jnp.bfloat16)


def on_device(tokens, expert_ids, gate_fixed, w_gate, w_up, w_down, cap=CAP):
    devices = lax.axis_size("expert")
    groups = lax.axis_size("tensor")
    token_count = tokens.shape[0]
    matched = expert_ids[:, :, None] == jnp.arange(EXPERTS, dtype=jnp.int32)
    routed = jnp.any(matched, axis=1)
    units = jnp.sum(jnp.where(matched, gate_fixed[:, :, None], 0), axis=1)
    order = jnp.arange(token_count, dtype=jnp.int32)
    earlier = (order[:, None] > order[None, :]).astype(jnp.bfloat16)
    position = jnp.dot(
        earlier, routed.astype(jnp.bfloat16), preferred_element_type=jnp.float32
    ).astype(jnp.int32)
    slots = jnp.arange(cap, dtype=jnp.int32)
    placed = (position[:, :, None] == slots) & routed[:, :, None]
    outgoing = jnp.einsum(
        "tec,td->ecd", placed.astype(jnp.bfloat16), tokens, preferred_element_type=jnp.float32
    ).astype(jnp.bfloat16)

    def selector(digit):
        chosen = jnp.where(placed, digit[:, :, None], 0).astype(jnp.bfloat16)
        return jnp.tile(chosen.reshape(token_count, EXPERTS * cap), (1, devices // EXPERTS))

    high, low = selector(units // 256), selector(units % 256)
    plan = along_line if groups <= LINE else by_collectives
    return plan(outgoing, high, low, w_gate, w_up, w_down, devices, groups, cap)


def solution(mesh):
    placed = (
        P("expert", "tensor"),
        P("expert", None),
        P("expert", None),
        P("expert", None, "tensor"),
        P("expert", None, "tensor"),
        P("expert", None, "tensor"),
    )
    return jax.shard_map(
        on_device, mesh=mesh, in_specs=placed, out_specs=P("expert", "tensor"), check_vma=False
    )
```

```python
import functools

import jax
import jax.numpy as jnp
from jax import lax
from jax.experimental import pallas as pl
from jax.experimental.pallas import tpu as pltpu
from jax.sharding import PartitionSpec as P

EXPERTS = 4
CAP = 48
MESH = pl.DeviceIdType.MESH
CHUNK = 256
SKEW = 2
LINE = 4
ORDER = {4: (0, 1, 2, 3), 8: (0, 1, 6, 7, 2, 3, 4, 5)}
CONTRACT_LAST = (((1,), (1,)), ((), ()))


def line_kernel(
    devices, groups, cap, chunk,
    outgoing, high, low, w_gate, w_up, w_down, mixed,
    gate_v, up_v, down_v, rows, running, term, hidden, total, returned,
    gate_sem, up_sem, down_sem, out_send, out_recv, back_send, back_recv,
    run_send, run_recv, hid_send, hid_recv,
):
    me, at = lax.axis_index("expert"), lax.axis_index("tensor")
    held = outgoing.shape[0]
    part = devices * cap // 4
    count = w_gate.shape[1] // chunk
    order = ORDER[devices]
    last = groups - 1
    place = (last - at, at)
    onward = (at - 1, at + 1)
    before = (at + 1, at - 1)
    ahead = jnp.minimum(place[0], place[1])
    behind = jnp.maximum(place[0], place[1])

    def weight(source, target, sem, c):
        cut = pl.ds(pl.multiple_of(c * chunk, chunk), chunk)
        return pltpu.make_async_copy(source.at[0, cut, :], target.at[cut, :], sem.at[c])

    def start_first(c, carry):
        weight(w_gate, gate_v, gate_sem, c).start()
        weight(w_up, up_v, up_sem, c).start()
        return carry

    def start_second(c, carry):
        weight(w_down, down_v, down_sem, c).start()
        return carry

    lax.fori_loop(0, count, start_first, 0)

    barrier = pltpu.get_barrier_semaphore()
    for k in range(1, devices):
        peer = lax.rem(me + k, devices)
        pl.semaphore_signal(barrier, inc=1, device_id={"expert": peer}, device_id_type=MESH)

    @pl.when(at > 0)
    def _():
        pl.semaphore_signal(barrier, inc=1, device_id={"tensor": at - 1}, device_id_type=MESH)

    @pl.when(at < last)
    def _():
        pl.semaphore_signal(barrier, inc=1, device_id={"tensor": at + 1}, device_id_type=MESH)

    inside = (at > 0) & (at < last)

    @pl.when(inside)
    def _():
        pl.semaphore_wait(barrier, devices + 1)

    @pl.when(jnp.logical_not(inside))
    def _():
        pl.semaphore_wait(barrier, devices - 1 + min(last, 1))

    def block(shard):
        return pl.ds(pl.multiple_of(shard * cap, cap), cap)

    def partner(slot):
        peer = 0
        for bit in (1, 2, 4):
            if bit < devices:
                peer += lax.rem(lax.div(me, bit) + order[slot] // bit % 2, 2) * bit
        return peer

    def dispatch(slot):
        peer = partner(slot)
        return pltpu.make_async_remote_copy(
            src_ref=outgoing.at[lax.rem(peer, held)],
            dst_ref=rows.at[slot * cap : (slot + 1) * cap, :],
            send_sem=out_send.at[slot],
            recv_sem=out_recv.at[slot],
            device_id={"expert": peer},
            device_id_type=MESH,
        )

    def back(slot):
        peer = partner(slot)
        return pltpu.make_async_remote_copy(
            src_ref=rows.at[slot * cap : (slot + 1) * cap, :],
            dst_ref=returned.at[block(me), :],
            send_sem=back_send.at[slot],
            recv_sem=back_recv.at[slot],
            device_id={"expert": peer},
            device_id_type=MESH,
        )

    for slot in range(1, devices):
        dispatch(slot).start()
    lax.fori_loop(0, count, start_second, 0)
    rows[:cap, :] = outgoing[lax.rem(me, held)]
    total[...] = jnp.zeros_like(total)
    for slot in range(1, devices // 2):
        dispatch(slot).wait_recv()

    def run_copy(s, c):
        return pltpu.make_async_remote_copy(
            src_ref=running.at[s, c],
            dst_ref=running.at[s, c],
            send_sem=run_send.at[s, c],
            recv_sem=run_recv.at[s, c],
            device_id={"tensor": onward[s]},
            device_id_type=MESH,
        )

    def hid_copy(s, c):
        return pltpu.make_async_remote_copy(
            src_ref=hidden.at[s, c],
            dst_ref=hidden.at[s, c],
            send_sem=hid_send.at[s, c],
            recv_sem=hid_recv.at[s, c],
            device_id={"tensor": before[s]},
            device_id_type=MESH,
        )

    def step(t, carry):
        fresh = t - SKEW * ahead

        @pl.when((fresh >= 0) & (fresh < count))
        def _():
            weight(w_gate, gate_v, gate_sem, fresh).wait()
            weight(w_up, up_v, up_sem, fresh).wait()

        @pl.when(fresh == count)
        def _():
            for slot in range(devices // 2, devices):
                dispatch(slot).wait_recv()

        for s in (0, 1):
            c = t - SKEW * place[s]

            @pl.when((c >= 0) & (c < 2 * count))
            def _(s=s, c=c):
                cut = pl.ds(pl.multiple_of(lax.rem(c, count) * chunk, chunk), chunk)
                group = 2 * lax.div(c, count) + s
                own = rows[pl.ds(pl.multiple_of(group * part, part), part), :]
                term[:, :chunk] = lax.dot_general(
                    own, gate_v[cut, :], CONTRACT_LAST, preferred_element_type=jnp.float32
                )
                term[:, chunk:] = lax.dot_general(
                    own, up_v[cut, :], CONTRACT_LAST, preferred_element_type=jnp.float32
                )

                @pl.when(place[s] == 0)
                def _():
                    running[s, c] = term[...].astype(jnp.bfloat16)
                    run_copy(s, c).start()

                @pl.when((place[s] > 0) & (place[s] < last))
                def _():
                    run_copy(s, c).wait_recv()
                    running[s, c] = (running[s, c].astype(jnp.float32) + term[...]).astype(
                        jnp.bfloat16
                    )
                    run_copy(s, c).start()

                @pl.when(place[s] == last)
                def _():
                    run_copy(s, c).wait_recv()
                    whole = running[s, c].astype(jnp.float32) + term[...]
                    gate, up = whole[:, :chunk], whole[:, chunk:]
                    hidden[s, c] = (gate / (1.0 + jnp.exp(-gate)) * up).astype(jnp.bfloat16)
                    hid_copy(s, c).start()

        for s in (0, 1):
            c = t - 2 * SKEW * last + SKEW * place[s]

            @pl.when((c >= 0) & (c < 2 * count) & (place[s] < last))
            def _(s=s, c=c):
                hid_copy(s, c).wait_recv()

                @pl.when(place[s] > 0)
                def _():
                    hid_copy(s, c).start()

        ripe = t - 2 * SKEW * last + SKEW * behind

        @pl.when((ripe >= 0) & (ripe < count))
        def _():
            weight(w_down, down_v, down_sem, ripe).wait()

        for s in (0, 1):
            c = t - 2 * SKEW * last + SKEW * place[s]

            @pl.when((c >= 0) & (c < 2 * count))
            def _(s=s, c=c):
                cut = pl.ds(pl.multiple_of(lax.rem(c, count) * chunk, chunk), chunk)
                total[2 * lax.div(c, count) + s] += jnp.dot(
                    hidden[s, c], down_v[cut, :], preferred_element_type=jnp.float32
                )

            for later in (0, 1):

                @pl.when(c == (later + 1) * count - 1)
                def _(group=2 * later + s):
                    rows[group * part : (group + 1) * part, :] = total[group].astype(jnp.bfloat16)
                    for slot in range(group * devices // 4, (group + 1) * devices // 4):
                        if slot > 0:
                            back(slot).start()

        return carry

    lax.fori_loop(0, 2 * count + 2 * SKEW * last, step, 0)
    returned[block(me), :] = rows[:cap, :]

    def drain(c, carry):
        for s in (0, 1):

            @pl.when(place[s] < last)
            def _(s=s):
                run_copy(s, c).wait_send()

            @pl.when(place[s] > 0)
            def _(s=s):
                hid_copy(s, c).wait_send()

        return carry

    lax.fori_loop(0, 2 * count, drain, 0)
    for slot in range(1, devices):
        dispatch(slot).wait_send()
    for slot in range(1, devices):
        peer = partner(slot)
        pltpu.make_async_remote_copy(
            src_ref=rows.at[slot * cap : (slot + 1) * cap, :],
            dst_ref=returned.at[block(peer), :],
            send_sem=back_send.at[slot],
            recv_sem=back_recv.at[slot],
            device_id={"expert": peer},
            device_id_type=MESH,
        ).wait_recv()
    coarse = jnp.zeros(mixed.shape, jnp.float32)
    fine = jnp.zeros(mixed.shape, jnp.float32)
    for q in range(devices // held):
        came = returned[q * held * cap : (q + 1) * held * cap, :]
        coarse += jnp.dot(high[...], came, preferred_element_type=jnp.float32)
        fine += jnp.dot(low[...], came, preferred_element_type=jnp.float32)
    mixed[...] = ((coarse * 256.0 + fine) * (1.0 / 65536.0)).astype(mixed.dtype)
    for slot in range(1, devices):
        back(slot).wait_send()


def along_line(outgoing, high, low, w_gate, w_up, w_down, devices, groups, cap):
    token_count, width_part = high.shape[0], outgoing.shape[2]
    hidden_width = w_gate.shape[1]
    chunk = min(CHUNK, hidden_width)
    count = hidden_width // chunk
    part = devices * cap // 4
    in_vmem, in_place = pl.BlockSpec(memory_space=pltpu.VMEM), pl.BlockSpec(memory_space=pl.ANY)
    flops = 2 * 3 * 4 * part * hidden_width * width_part
    return pl.pallas_call(
        functools.partial(line_kernel, devices, groups, cap, chunk),
        out_shape=jax.ShapeDtypeStruct((token_count, width_part), jnp.bfloat16),
        in_specs=[in_vmem] * 3 + [in_place] * 3,
        out_specs=in_vmem,
        scratch_shapes=[
            pltpu.VMEM((hidden_width, width_part), jnp.bfloat16),
            pltpu.VMEM((hidden_width, width_part), jnp.bfloat16),
            pltpu.VMEM((hidden_width, width_part), jnp.bfloat16),
            pltpu.VMEM((4 * part, width_part), jnp.bfloat16),
            pltpu.VMEM((2, 2 * count, part, 2 * chunk), jnp.bfloat16),
            pltpu.VMEM((part, 2 * chunk), jnp.float32),
            pltpu.VMEM((2, 2 * count, part, chunk), jnp.bfloat16),
            pltpu.VMEM((4, part, width_part), jnp.float32),
            pltpu.VMEM((4 * part, width_part), jnp.bfloat16),
            *[pltpu.SemaphoreType.DMA((count,))] * 3,
            *[pltpu.SemaphoreType.DMA((devices,))] * 4,
            *[pltpu.SemaphoreType.DMA((2, 2 * count))] * 4,
        ],
        compiler_params=pltpu.CompilerParams(
            collective_id=0, has_side_effects=True, vmem_limit_bytes=60 * 2**20
        ),
        cost_estimate=pl.CostEstimate(
            flops=flops,
            bytes_accessed=3 * 2 * hidden_width * width_part,
            transcendentals=2 * part * hidden_width,
        ),
    )(outgoing, high, low, w_gate, w_up, w_down)


def by_collectives(outgoing, high, low, w_gate, w_up, w_down, devices, groups, cap):
    width_part = outgoing.shape[2]
    arrived = lax.all_to_all(
        jnp.tile(outgoing, (devices // EXPERTS, 1, 1)), "expert", split_axis=0, concat_axis=0, tiled=True
    )
    total_rows = devices * cap
    rows_in = arrived.reshape(total_rows, width_part)
    hidden_width = w_gate.shape[1]

    def summed(weights):
        product = lax.dot_general(
            rows_in, weights[0], CONTRACT_LAST, preferred_element_type=jnp.float32
        ).astype(jnp.bfloat16)
        parts = lax.all_to_all(product, "tensor", split_axis=0, concat_axis=0, tiled=True)
        parts = parts.reshape(groups, total_rows // groups, hidden_width)
        return jnp.sum(parts.astype(jnp.float32), axis=0)

    hidden = (jax.nn.silu(summed(w_gate)) * summed(w_up)).astype(jnp.bfloat16)
    partial_out = jnp.dot(
        lax.all_gather(hidden, "tensor", axis=0, tiled=True),
        w_down[0],
        preferred_element_type=jnp.float32,
    )
    returned = lax.all_to_all(
        partial_out.reshape(devices, cap, width_part), "expert", split_axis=0, concat_axis=0, tiled=True
    )
    selector = (high.astype(jnp.float32) * 256.0 + low.astype(jnp.float32)) / 65536.0
    selector = jnp.tile(selector, (1, devices // EXPERTS))
    mixed = jnp.dot(
        selector, returned.reshape(total_rows, width_part), precision=lax.Precision.HIGHEST
    )
    return mixed.astype(jnp.bfloat16)


def on_device(tokens, expert_ids, gate_fixed, w_gate, w_up, w_down, cap=CAP):
    devices = lax.axis_size("expert")
    groups = lax.axis_size("tensor")
    token_count = tokens.shape[0]
    matched = expert_ids[:, :, None] == jnp.arange(EXPERTS, dtype=jnp.int32)
    routed = jnp.any(matched, axis=1)
    units = jnp.sum(jnp.where(matched, gate_fixed[:, :, None], 0), axis=1)
    order = jnp.arange(token_count, dtype=jnp.int32)
    earlier = (order[:, None] > order[None, :]).astype(jnp.bfloat16)
    position = jnp.dot(
        earlier, routed.astype(jnp.bfloat16), preferred_element_type=jnp.float32
    ).astype(jnp.int32)
    column = jnp.arange(EXPERTS * cap, dtype=jnp.int32)
    target = jnp.where(routed, position + cap * jnp.arange(EXPERTS, dtype=jnp.int32), -1)

    def spread(values):
        chosen = [jnp.where(column == target[:, e : e + 1], values[:, e : e + 1], 0) for e in range(EXPERTS)]
        return sum(chosen).astype(jnp.bfloat16)

    outgoing = lax.dot_general(
        spread(routed.astype(jnp.int32)), tokens, (((0,), (0,)), ((), ())), preferred_element_type=jnp.float32
    ).astype(jnp.bfloat16)
    outgoing = outgoing.reshape(EXPERTS, cap, tokens.shape[1])
    high, low = spread(units // 256), spread(units % 256)
    plan = along_line if groups <= LINE and devices in ORDER else by_collectives
    return plan(outgoing, high, low, w_gate, w_up, w_down, devices, groups, cap)


def solution(mesh):
    placed = (
        P("expert", "tensor"),
        P("expert", None),
        P("expert", None),
        P("expert", None, "tensor"),
        P("expert", None, "tensor"),
        P("expert", None, "tensor"),
    )
    return jax.shard_map(
        on_device, mesh=mesh, in_specs=placed, out_specs=P("expert", "tensor"), check_vma=False
    )
```
